512 devices in a mesh: tm: 4 (over y_lo, core), lat: 4 (over y_hi), lon: 32 (over z, x).
Axes of the slice: x: 4, y: 8 (y_hi: 4, y_lo: 2; y = y_hi * 2 + y_lo), z: 8, core: 2. Of those that a mesh axis runs over, the one named last changes fastest.
Arguments:
- state: bfloat16 [4, 4, 137, 32, 8192], P('tm', None, None, 'lat', 'lon'), may hold values from -6 to 6
- band_counts: int32 [4, 4], P('tm', 'lat'), may hold values from 2 to 6
- dep_blocks: int32 [4, 32, 64, 6], P('tm', 'lat', 'lon'), may hold values from 0 to 63, as said below
- lon_entry: int32 [4, 32, 8192], P('tm', 'lat', 'lon'), may hold values from 0 to 5
- lon_offset: int32 [4, 32, 8192], P('tm', 'lat', 'lon'), may hold values from 1 to 125
- lon_frac: float32 [4, 32, 8192], P('tm', 'lat', 'lon'), may hold values from 0 to 1
- lat_offset: int32 [4, 32, 8192], P('tm', 'lat', 'lon'), may hold values from -1 to 0
- lat_frac: float32 [4, 32, 8192], P('tm', 'lat', 'lon'), may hold values from 0 to 1
Outputs:
- misfit: bfloat16 [4, 4, 137, 32, 8192], P('tm', None, None, 'lat', 'lon')
The draws below stay inside these ranges and needn't reach their ends.
Inputs may be any that keep to these rules, and one draw needn't show every extreme that they name: `dep_blocks`: the list of a destination block names each of the 6 blocks of its latitude row that lie from 3 blocks west of the first block of the destination's tile to 1 block east of the tile's last block (block numbers taken modulo 64) exactly once, in an order drawn for each block.
All inputs are finite; a program needn't handle non-finite values.
Results may differ from the reference program's by a relative error of at most 0.0046.
Values may be sent and summed in bfloat16 or wider, within the bound.
No kernel may reach another device: no remote copies, remote signals or barrier semaphores. Data moves between devices by JAX's collectives and lax.ppermute only.
A program may use at most 64 MiB of HBM per device.

```python
import jax
import jax.numpy as jnp
from jax import lax

VARS = 4
LEV = 137
BLK = 128
NB = 2
RL = 8
KMAX = 6
WINDOWS = 4
BANDS = 4
NROWS = 32
CYCLE = 64
COLS = 8192


def draw_dep_blocks(key, part):
    keyed = jax.random.fold_in(jax.random.fold_in(key, 202), part)
    scores = jax.random.randint(jax.random.fold_in(keyed, 21), (WINDOWS, NROWS, CYCLE, KMAX), 0, 2 ** 20, dtype=jnp.int32)
    scores = scores * KMAX + jnp.arange(KMAX, dtype=jnp.int32)
    ordering = jnp.argsort(scores, axis=-1, stable=True).astype(jnp.int32)
    block_index = jnp.arange(CYCLE, dtype=jnp.int32)
    tile_start = block_index // NB * NB
    return ((tile_start[None, None, :, None] - NB - NB // 2 + ordering) % CYCLE).astype(jnp.int32)


def place_ends(entries, key, smallest, top_value):
    place = [jax.random.randint(jax.random.fold_in(key, axis), (), 0, length) for axis, length in enumerate(entries.shape)]
    longest = entries.shape.index(max(entries.shape))
    neighbour = place[:longest] + [(place[longest] + 1) % entries.shape[longest]] + place[longest + 1:]
    return entries.at[tuple(place)].set(smallest).at[tuple(neighbour)].set(top_value)


def block_scale(stream_key, shape, split, least, top_value):
    level, own = 1.0, jax.random.fold_in(stream_key, 6)
    for dim, parts in split:
        heights = jnp.exp(jax.random.uniform(jax.random.fold_in(own, dim), (parts,), jnp.float32, least / len(split), top_value / len(split)))
        level = level * jnp.repeat(heights, shape[dim] // parts).reshape([-1 if axis == dim else 1 for axis in range(len(shape))])
    return level


def gaussian(rng, dims, spread, bound, cuts=(), kind=jnp.bfloat16):
    factor_of = block_scale(rng, dims, cuts, -0.22, 0.18) if cuts else 1.0
    result = jax.random.normal(rng, dims, jnp.float32) * spread * factor_of
    return jnp.minimum(jnp.maximum(result, -bound), bound).astype(kind)


def setup_inputs(seed: int = 0) -> dict:
    splits = jax.random.split(jax.random.key(seed), 9)
    state = gaussian(splits[0], (WINDOWS, VARS, LEV, NROWS, COLS), 1.0, 6.0, ((0, 4), (3, 4), (4, 32)))
    band_counts = place_ends(jax.random.randint(splits[1], (WINDOWS, BANDS), 2, KMAX + 1), jax.random.fold_in(splits[1], 1), 2, KMAX).astype(jnp.int32)
    dep_blocks = draw_dep_blocks(jax.random.fold_in(splits[8], 71), 0)
    lon_entry = place_ends(jax.random.randint(splits[3], (WINDOWS, NROWS, COLS), 0, KMAX), jax.random.fold_in(splits[3], 1), 0, KMAX - 1).astype(jnp.int32)
    lon_offset = place_ends(jax.random.randint(splits[4], (WINDOWS, NROWS, COLS), 1, BLK - 2), jax.random.fold_in(splits[4], 1), 1, (BLK - 2) - 1).astype(jnp.int32)
    lon_frac = jnp.clip(1.0 * jax.random.uniform(splits[5], (WINDOWS, NROWS, COLS), jnp.float32) ** block_scale(splits[5], (WINDOWS, NROWS, COLS), ((0, 4), (1, 4), (2, 32)), -0.2, 0.2), 0.0, 1.0)
    lat_offset = place_ends(jax.random.randint(splits[6], (WINDOWS, NROWS, COLS), -1, 1), jax.random.fold_in(splits[6], 1), -1, 0).astype(jnp.int32)
    lat_frac = jnp.clip(1.0 * jax.random.uniform(splits[7], (WINDOWS, NROWS, COLS), jnp.float32) ** block_scale(splits[7], (WINDOWS, NROWS, COLS), ((0, 4), (1, 4), (2, 32)), -0.2, 0.2), 0.0, 1.0)
    return {"state": state, "band_counts": band_counts, "dep_blocks": dep_blocks, "lon_entry": lon_entry, "lon_offset": lon_offset, "lon_frac": lon_frac, "lat_offset": lat_offset, "lat_frac": lat_frac}


def cubic_weights(fraction):
    return jnp.stack([
        -fraction * (fraction - 1.0) * (fraction - 2.0) / 6.0,
        (fraction + 1.0) * (fraction - 1.0) * (fraction - 2.0) / 2.0,
        -(fraction + 1.0) * fraction * (fraction - 2.0) / 2.0,
        (fraction + 1.0) * fraction * (fraction - 1.0) / 6.0,
    ])


def reference(state, band_counts, dep_blocks, lon_entry, lon_offset, lon_frac, lat_offset, lat_frac):
    depth_rows = VARS * LEV
    windows = state.reshape(WINDOWS, depth_rows, NROWS, COLS)
    band_of_row = jnp.arange(NROWS, dtype=jnp.int32) // RL
    block_of_col = jnp.arange(COLS, dtype=jnp.int32) // BLK
    stencil_nodes = jnp.arange(4, dtype=jnp.int32)

    def one_window(previous, window):
        fields, counts, departure_lists, entry_rows, offset_rows, fraction_rows, lat_shift, lat_fraction = window
        by_row = jnp.swapaxes(fields, 0, 1)

        def one_row(row_data):
            source_row, list_row, entry_row, offset_row, fraction_row, band_index = row_data
            entry_slot = entry_row % counts[band_index]
            chosen = jnp.take_along_axis(list_row[block_of_col], entry_slot[:, None], axis=1)[:, 0]
            positions = (chosen[:, None] * BLK + offset_row[:, None] - 1 + stencil_nodes[None, :]).astype(jnp.int32)
            rounded = lax.optimization_barrier(cubic_weights(fraction_row).astype(jnp.bfloat16))
            weights = rounded.astype(jnp.float32)
            picked = source_row[:, positions].astype(jnp.float32)
            return jnp.sum(picked * weights.T[None, :, :], axis=2).astype(jnp.bfloat16)

        advected = lax.map(one_row, (by_row, departure_lists, entry_rows, offset_rows, fraction_rows, band_of_row))
        padded = jnp.pad(advected, ((2, 2), (0, 0), (0, 0)))
        lat_weights = cubic_weights(lat_fraction)
        end_sum = jnp.zeros((NROWS, depth_rows, COLS), jnp.float32)
        for shift_rows in range(-2, 3):
            coefficient = jnp.zeros((NROWS, COLS), jnp.float32)
            for node_index in range(4):
                coefficient = coefficient + jnp.where(lat_shift + node_index - 1 == shift_rows, lat_weights[node_index], 0.0)
            end_sum = end_sum + coefficient[:, None, :] * padded[2 + shift_rows:2 + shift_rows + NROWS].astype(jnp.float32)
        end_state = end_sum.astype(jnp.bfloat16)
        misfit_rows = (by_row.astype(jnp.float32) - previous.astype(jnp.float32)).astype(jnp.bfloat16)
        return end_state, misfit_rows

    start = jnp.zeros((NROWS, depth_rows, COLS), jnp.bfloat16)
    _, misfits = lax.scan(one_window, start, (windows, band_counts, dep_blocks, lon_entry, lon_offset, lon_frac, lat_offset, lat_frac))
    return jnp.swapaxes(misfits, 1, 2).reshape(WINDOWS, VARS, LEV, NROWS, COLS)
```

```python
import functools

import jax
import jax.numpy as jnp
from jax import lax
from jax.experimental import pallas as pl
from jax.experimental.pallas import tpu as pltpu
from jax.sharding import PartitionSpec as P

BLK = 128
AXES = ("tm", "lat", "lon")
VMEM_LIMIT = 16 * 1024 * 1024
VMEM = pl.BlockSpec(memory_space=pltpu.VMEM)


def params():
    return pltpu.CompilerParams(vmem_limit_bytes=VMEM_LIMIT)


def cubic(s):
    return (
        -s * (s - 1.0) * (s - 2.0) / 6.0,
        (s + 1.0) * (s - 1.0) * (s - 2.0) / 2.0,
        -(s + 1.0) * s * (s - 2.0) / 2.0,
        (s + 1.0) * s * (s - 1.0) / 6.0,
    )


def move(value, dest, windows):
    bands, tiles = lax.axis_size("lat"), lax.axis_size("lon")
    pairs = []
    for t in windows:
        for b in range(bands):
            for j in range(tiles):
                to = dest(t, b, j)
                if to is not None:
                    source = (t * bands + b) * tiles + j
                    pairs.append((source, (to[0] * bands + to[1]) * tiles + to[2]))
    return lax.ppermute(value, AXES, pairs)


def split_kernel(x_ref, whole_ref, west_ref, east_ref, *wide):
    depth, rows, cols = x_ref.shape
    padded = whole_ref.shape[1]
    for g, (half_ref, buf) in enumerate(zip((west_ref, east_ref), wide)):
        lanes = slice(g * BLK, (g + 1) * BLK)
        buf[: depth * rows] = x_ref[:, :, lanes].astype(jnp.float32).reshape(depth * rows, BLK)
        if padded > depth:
            buf[depth * rows :] = jnp.zeros(((padded - depth) * rows, BLK), jnp.float32)
        for r in range(rows):
            slab = buf[pl.ds(r, padded, stride=rows), :].astype(jnp.bfloat16)
            whole_ref[r, :, lanes] = slab
            half_ref[r] = slab


def split_rows(x):
    _, rows, cols = x.shape
    depth = -(-x.shape[0] // 16) * 16
    bf16 = jnp.bfloat16
    return pl.pallas_call(
        split_kernel,
        out_shape=(
            jax.ShapeDtypeStruct((rows, depth, cols), bf16),
            jax.ShapeDtypeStruct((rows, depth, cols // 2), bf16),
            jax.ShapeDtypeStruct((rows, depth, cols // 2), bf16),
        ),
        in_specs=[VMEM],
        out_specs=(VMEM, VMEM, VMEM),
        scratch_shapes=[pltpu.VMEM((depth * rows, BLK), jnp.float32)] * 2,
        compiler_params=params(),
        cost_estimate=pl.CostEstimate(flops=0, bytes_accessed=6 * x.size, transcendentals=0),
        name="split_rows",
    )(x)


def matrix_kernel(geo_ref, m_ref):
    r = pl.program_id(0)
    _, span, cols = m_ref.shape
    first = geo_ref[0, pl.ds(r, 1), :].astype(jnp.int32)
    weights = [w.astype(jnp.bfloat16).astype(jnp.float32) for w in cubic(geo_ref[1, pl.ds(r, 1), :])]
    step = BLK // 2
    for s in range(0, span, step):
        gap = lax.broadcasted_iota(jnp.int32, (step, cols), 0) - (first - s)
        value = jnp.where(gap == 0, weights[0], 0.0)
        for node in range(1, 4):
            value = jnp.where(gap == node, weights[node], value)
        m_ref[0, s : s + step, :] = value.astype(jnp.bfloat16)


def matrices(geo, span):
    _, rows, cols = geo.shape
    return pl.pallas_call(
        matrix_kernel,
        grid=(rows,),
        out_shape=jax.ShapeDtypeStruct((rows, span, cols), jnp.bfloat16),
        in_specs=[pl.BlockSpec(geo.shape, lambda r: (0, 0, 0))],
        out_specs=pl.BlockSpec((1, span, cols), lambda r: (r, 0, 0)),
        compiler_params=params(),
        cost_estimate=pl.CostEstimate(
            flops=9 * rows * span * cols, bytes_accessed=2 * rows * span * cols, transcendentals=0
        ),
        name="matrices",
    )(geo)


def row_product(far, near, west, own, m):
    outer = jnp.concatenate([far, near], axis=1)
    k = outer.shape[1]
    f32 = jnp.float32
    total = jnp.dot(outer, m[:k], preferred_element_type=f32)
    total += jnp.dot(west, m[k : 2 * k], preferred_element_type=f32)
    total += jnp.dot(own, m[2 * k :], preferred_element_type=f32)
    return total.astype(jnp.bfloat16)


def lon_kernel(*refs, per_step):
    ins, outs = refs[: 5 * per_step], refs[len(refs) - per_step :]
    for k in range(per_step):
        far, near, west, own, m = ins[5 * k : 5 * k + 5]
        outs[k][0] = row_product(far[0], near[0], west[0], own[0], m[0])


def lon_rows(far, near, west, own, m, firsts, count, after=()):
    _, depth, cols = own.shape
    arrays = (far, near, west, own, m)

    def at(array, first):
        return pl.BlockSpec((1,) + array.shape[1:], lambda i, first=first: (i + first, 0, 0))

    return pl.pallas_call(
        functools.partial(lon_kernel, per_step=len(firsts)),
        grid=(count,),
        out_shape=[jax.ShapeDtypeStruct((count, depth, cols), jnp.bfloat16) for _ in firsts],
        in_specs=[at(array, first) for first in firsts for array in arrays]
        + [pl.BlockSpec(memory_space=pl.ANY)] * len(after),
        out_specs=[pl.BlockSpec((1, depth, cols), lambda i: (i, 0, 0)) for _ in firsts],
        compiler_params=params(),
        cost_estimate=pl.CostEstimate(
            flops=2 * len(firsts) * count * depth * m.shape[1] * cols,
            bytes_accessed=2 * len(firsts) * count * (4 * depth * cols + m.shape[1] * cols),
            transcendentals=0,
        ),
        name="lon_rows",
    )(*(arrays * len(firsts)), *after)


def lat_kernel(above, top, mid, bot, below, geo_ref, out_ref, *wide):
    depth, rows, cols = out_ref.shape
    chunk = 48
    shift, weights = geo_ref[2].astype(jnp.int32), cubic(geo_ref[3])
    coefficients = []
    for distance in range(-2, 3):
        total = jnp.zeros_like(weights[0])
        for node in range(4):
            total += jnp.where(shift + node - 1 == distance, weights[node], 0.0)
        coefficients.append(total)
    padded = [(ref, i) for ref in (above, top, mid, bot, below) for i in range(ref.shape[0])]
    for low in range(0, depth, chunk):
        size = min(chunk, depth - low)
        for r in range(rows):
            total = None
            for k in range(5):
                ref, i = padded[r + k]
                term = coefficients[k][r : r + 1] * ref[i, low : low + size, :].astype(jnp.float32)
                total = term if total is None else total + term
            for g, buf in enumerate(wide):
                buf[pl.ds(low * rows + r, size, stride=rows), :] = total[:, g * BLK : (g + 1) * BLK]
        for g, buf in enumerate(wide):
            block = buf[low * rows : (low + size) * rows, :].astype(jnp.bfloat16)
            out_ref[low : low + size, :, g * BLK : (g + 1) * BLK] = block.reshape(size, rows, BLK)


def lat_rows(above, top, mid, bot, below, geo, depth):
    cols = mid.shape[2]
    rows = geo.shape[1]
    return pl.pallas_call(
        lat_kernel,
        out_shape=jax.ShapeDtypeStruct((depth, rows, cols), jnp.bfloat16),
        in_specs=[VMEM] * 6,
        out_specs=VMEM,
        scratch_shapes=[pltpu.VMEM((depth * rows, BLK), jnp.float32)] * (cols // BLK),
        compiler_params=params(),
        cost_estimate=pl.CostEstimate(
            flops=10 * depth * rows * cols, bytes_accessed=5 * depth * rows * cols, transcendentals=0
        ),
        name="lat_rows",
    )(above, top, mid, bot, below, geo)


def geometry(band_counts, dep_blocks, lon_entry, lon_offset, lon_frac, lat_offset, lat_frac):
    blocks, kmax = dep_blocks.shape[2:]
    cycle = blocks * lax.axis_size("lon")
    count, entry = band_counts[0, 0], lon_entry[0]
    slot = entry % count
    place = (dep_blocks[0] - lax.axis_index("lon") * blocks + blocks + blocks // 2) % cycle
    place = jnp.where(place == 0, 0, jnp.where(place == 3 * blocks - 1, 1, place + 1))
    place = jnp.repeat(place, BLK, axis=1)
    chosen = place[:, :, 0]
    for k in range(1, kmax):
        chosen = jnp.where(slot == k, place[:, :, k], chosen)
    first = chosen * BLK + lon_offset[0] - 1
    return jnp.stack(
        [first.astype(jnp.float32), lon_frac[0], lat_offset[0].astype(jnp.float32), lat_frac[0]]
    )


def body(state, *rest):
    fields_n, levels, rows, cols = state.shape[1:]
    depth = fields_n * levels
    windows, bands, tiles = (lax.axis_size(a) for a in AXES)
    flat = state.reshape(depth, rows, cols)
    cut = depth // 32 * 16
    tm = lax.axis_index("tm")

    def lend(t, b, j):
        return (3, b, j)

    geo_own = geometry(*rest)
    geo = jnp.where(tm == 3, move(geo_own, lend, (1,)), geo_own)
    second = jnp.where(tm == 3, move(flat[cut:], lend, (1,)), flat[cut:])
    m = matrices(geo, 3 * cols)

    ends, after = [], ()
    parts = (
        (flat[:cut], (0, 1, 2), {0: 1, 1: 2, 2: 3}),
        (second, (0, 2, 3), {0: 1, 3: 2, 2: 3}),
    )
    for part, active, onward in parts:
        own, west_half, east_half = split_rows(part)
        west = move(own, lambda t, b, j: (t, b, (j + 1) % tiles), active)
        near = move(west_half, lambda t, b, j: (t, b, (j - 1) % tiles), active)
        far = move(east_half, lambda t, b, j: (t, b, (j + 2) % tiles), active)
        top, bot = lon_rows(far, near, west, own, m, (0, rows - 2), 2, after)
        above = move(bot, lambda t, b, j: (t, b + 1, j) if b + 1 < bands else None, active)
        below = move(top, lambda t, b, j: (t, b - 1, j) if b > 0 else None, active)
        (mid,) = lon_rows(far, near, west, own, m, (2,), rows - 4)
        after = (mid,)
        end = lat_rows(above, top, mid, bot, below, geo, part.shape[0])
        ends.append(move(end, lambda t, b, j: (onward[t], b, j), active))
    previous = jnp.concatenate(ends, axis=0)
    misfit = (flat.astype(jnp.float32) - previous.astype(jnp.float32)).astype(jnp.bfloat16)
    return misfit.reshape(state.shape)


def solution(mesh):
    placed = (
        P("tm", None, None, "lat", "lon"),
        P("tm", "lat"),
        P("tm", "lat", "lon", None),
        P("tm", "lat", "lon"),
        P("tm", "lat", "lon"),
        P("tm", "lat", "lon"),
        P("tm", "lat", "lon"),
        P("tm", "lat", "lon"),
    )
    return jax.shard_map(
        body,
        mesh=mesh,
        in_specs=placed,
        out_specs=P("tm", None, None, "lat", "lon"),
        check_vma=False,
    )
```

```python
import functools

import jax
import jax.numpy as jnp
from jax import lax
from jax.experimental import pallas as pl
from jax.experimental.pallas import tpu as pltpu
from jax.sharding import PartitionSpec as P

BLK = 128
AXES = ("tm", "lat", "lon")
VMEM_LIMIT = 14 * 1024 * 1024
SHORT = pl.CostEstimate(flops=1000, bytes_accessed=1000, transcendentals=0)
VMEM = pl.BlockSpec(memory_space=pltpu.VMEM)


def params():
    return pltpu.CompilerParams(vmem_limit_bytes=VMEM_LIMIT)


def cubic(s):
    return (
        -s * (s - 1.0) * (s - 2.0) / 6.0,
        (s + 1.0) * (s - 1.0) * (s - 2.0) / 2.0,
        -(s + 1.0) * s * (s - 2.0) / 2.0,
        (s + 1.0) * s * (s - 1.0) / 6.0,
    )


def move(value, dest, windows):
    bands, tiles = lax.axis_size("lat"), lax.axis_size("lon")
    pairs = []
    for t in windows:
        for b in range(bands):
            for j in range(tiles):
                to = dest(t, b, j)
                if to is not None:
                    source = (t * bands + b) * tiles + j
                    pairs.append((source, (to[0] * bands + to[1]) * tiles + to[2]))
    return lax.ppermute(value, AXES, pairs)


def split_kernel(x_ref, *refs, picked):
    whole_ref, west_ref, east_ref, *wide = refs[-5:]
    depth, rows, cols = x_ref.shape
    padded = whole_ref.shape[1]
    for g, (half_ref, buf) in enumerate(zip((west_ref, east_ref), wide)):
        lanes = slice(g * BLK, (g + 1) * BLK)
        buf[: depth * rows] = x_ref[:, :, lanes].astype(jnp.float32).reshape(depth * rows, BLK)
        if padded > depth:
            buf[depth * rows :] = jnp.zeros(((padded - depth) * rows, BLK), jnp.float32)
        for i, r in enumerate(picked):
            slab = buf[pl.ds(r, padded, stride=rows), :].astype(jnp.bfloat16)
            whole_ref[i, :, lanes] = slab
            half_ref[i] = slab


def split_rows(x, picked, padded, after=()):
    depth, rows, cols = x.shape
    n = len(picked)
    half = jax.ShapeDtypeStruct((n, padded, cols // 2), x.dtype)
    return pl.pallas_call(
        functools.partial(split_kernel, picked=picked),
        out_shape=(jax.ShapeDtypeStruct((n, padded, cols), x.dtype), half, half),
        in_specs=[VMEM] + [pl.BlockSpec(memory_space=pl.ANY)] * len(after),
        out_specs=(VMEM, VMEM, VMEM),
        scratch_shapes=[pltpu.VMEM((padded * rows, BLK), jnp.float32)] * 2,
        compiler_params=params(),
        cost_estimate=SHORT,
        name="split_rows",
    )(x, *after)


def choose_kernel(lent_flag, lent_ref, own_ref, own_east_ref, *refs):
    whole_ref, west_ref, east_ref = refs[-3:]
    half = west_ref.shape[2]
    east_ref[...] = own_east_ref[...]

    def put(ref):
        for r in range(whole_ref.shape[0]):
            slab = ref[r]
            whole_ref[r] = slab
            west_ref[r] = slab[:, :half]

    @pl.when(lent_flag[0] == 1)
    def _():
        put(lent_ref)

    @pl.when(lent_flag[0] == 0)
    def _():
        put(own_ref)


def choose(flag, lent, own, own_east, after):
    half = jax.ShapeDtypeStruct(own_east.shape, own.dtype)
    return pl.pallas_call(
        choose_kernel,
        out_shape=(jax.ShapeDtypeStruct(own.shape, own.dtype), half, half),
        in_specs=[pl.BlockSpec(memory_space=pltpu.SMEM), VMEM, VMEM, VMEM]
        + [pl.BlockSpec(memory_space=pl.ANY)] * len(after),
        out_specs=(VMEM, VMEM, VMEM),
        compiler_params=params(),
        cost_estimate=SHORT,
        name="choose",
    )(flag, lent, own, own_east, *after)


def matrix_kernel(geo_ref, m_ref):
    r = pl.program_id(0)
    _, span, cols = m_ref.shape
    first = geo_ref[0, pl.ds(r, 1), :].astype(jnp.int32)
    weights = [w.astype(jnp.bfloat16).astype(jnp.float32) for w in cubic(geo_ref[1, pl.ds(r, 1), :])]
    step = BLK // 2
    for s in range(0, span, step):
        gap = lax.broadcasted_iota(jnp.int32, (step, cols), 0) - (first - s)
        value = jnp.where(gap == 0, weights[0], 0.0)
        for node in range(1, 4):
            value = jnp.where(gap == node, weights[node], value)
        m_ref[0, s : s + step, :] = value.astype(jnp.bfloat16)


def matrices(geo, span):
    _, rows, cols = geo.shape
    return pl.pallas_call(
        matrix_kernel,
        grid=(rows,),
        out_shape=jax.ShapeDtypeStruct((rows, span, cols), jnp.bfloat16),
        in_specs=[pl.BlockSpec(geo.shape, lambda r: (0, 0, 0))],
        out_specs=pl.BlockSpec((1, span, cols), lambda r: (r, 0, 0)),
        compiler_params=params(),
        cost_estimate=SHORT,
        name="matrices",
    )(geo)


def row_product(far, near, west, own, m):
    outer = jnp.concatenate([far, near], axis=1)
    k = outer.shape[1]
    f32 = jnp.float32
    total = jnp.dot(outer, m[:k], preferred_element_type=f32)
    total += jnp.dot(west, m[k : 2 * k], preferred_element_type=f32)
    total += jnp.dot(own, m[2 * k :], preferred_element_type=f32)
    return total.astype(jnp.bfloat16)


def lon_kernel(lent_flag, *refs, per_step):
    ins, outs = refs[: 6 * per_step], refs[len(refs) - per_step :]
    lent = lent_flag[0] == 1
    for k in range(per_step):
        far, far_lent, near, west, own, m = ins[6 * k : 6 * k + 6]
        second_west = jnp.where(lent, far_lent[0], far[0])
        outs[k][0] = row_product(second_west, near[0], west[0], own[0], m[0])


def lon_rows(flag, far, far_lent, near, west, own, m, firsts, count, after=()):
    _, depth, cols = own.shape
    arrays = (far, far_lent, near, west, own)

    def at(array, first):
        return pl.BlockSpec((1,) + array.shape[1:], lambda i, first=first: (i + first, 0, 0))

    specs = []
    for slab, row in firsts:
        specs += [at(array, slab) for array in arrays] + [at(m, row)]
    return pl.pallas_call(
        functools.partial(lon_kernel, per_step=len(firsts)),
        grid=(count,),
        out_shape=[jax.ShapeDtypeStruct((count, depth, cols), jnp.bfloat16) for _ in firsts],
        in_specs=[pl.BlockSpec(memory_space=pltpu.SMEM)] + specs + [pl.BlockSpec(memory_space=pl.ANY)] * len(after),
        out_specs=[pl.BlockSpec((1, depth, cols), lambda i: (i, 0, 0)) for _ in firsts],
        compiler_params=params(),
        cost_estimate=SHORT,
        name="lon_rows",
    )(flag, *((*arrays, m) * len(firsts)), *after)


def lat_kernel(above, top, mid, bot, below, geo_ref, out_ref, *wide):
    depth, rows, cols = out_ref.shape
    chunk = 48
    shift, weights = geo_ref[2].astype(jnp.int32), cubic(geo_ref[3])
    coefficients = []
    for distance in range(-2, 3):
        total = jnp.zeros_like(weights[0])
        for node in range(4):
            total += jnp.where(shift + node - 1 == distance, weights[node], 0.0)
        coefficients.append(total)
    padded = [(ref, i) for ref in (above, top, mid, bot, below) for i in range(ref.shape[0])]
    for low in range(0, depth, chunk):
        size = min(chunk, depth - low)
        for r in range(rows):
            total = None
            for k in range(5):
                ref, i = padded[r + k]
                term = coefficients[k][r : r + 1] * ref[i, low : low + size, :].astype(jnp.float32)
                total = term if total is None else total + term
            for g, buf in enumerate(wide):
                buf[pl.ds(low * rows + r, size, stride=rows), :] = total[:, g * BLK : (g + 1) * BLK]
        for g, buf in enumerate(wide):
            block = buf[low * rows : (low + size) * rows, :].astype(jnp.bfloat16)
            out_ref[low : low + size, :, g * BLK : (g + 1) * BLK] = block.reshape(size, rows, BLK)


def lat_rows(above, top, mid, bot, below, geo, depth):
    cols = mid.shape[2]
    rows = geo.shape[1]
    return pl.pallas_call(
        lat_kernel,
        out_shape=jax.ShapeDtypeStruct((depth, rows, cols), jnp.bfloat16),
        in_specs=[VMEM] * 6,
        out_specs=VMEM,
        scratch_shapes=[pltpu.VMEM((depth * rows, BLK), jnp.float32)] * (cols // BLK),
        compiler_params=params(),
        cost_estimate=SHORT,
        name="lat_rows",
    )(above, top, mid, bot, below, geo)


def geometry(band_counts, dep_blocks, lon_entry, lon_offset, lon_frac, lat_offset, lat_frac):
    blocks, kmax = dep_blocks.shape[2:]
    cycle = blocks * lax.axis_size("lon")
    count, entry = band_counts[0, 0], lon_entry[0]
    slot = entry % count
    place = (dep_blocks[0] - lax.axis_index("lon") * blocks + blocks + blocks // 2) % cycle
    place = jnp.where(place == 0, 0, jnp.where(place == 3 * blocks - 1, 1, place + 1))
    place = jnp.repeat(place, BLK, axis=1)
    chosen = place[:, :, 0]
    for k in range(1, kmax):
        chosen = jnp.where(slot == k, place[:, :, k], chosen)
    first = chosen * BLK + lon_offset[0] - 1
    return jnp.stack(
        [first.astype(jnp.float32), lon_frac[0], lat_offset[0].astype(jnp.float32), lat_frac[0]]
    )


def body(state, *rest):
    fields_n, levels, rows, cols = state.shape[1:]
    depth = fields_n * levels
    padded = -(-depth // 8) * 8
    _, bands, tiles = (lax.axis_size(a) for a in AXES)
    flat = state.reshape(depth, rows, cols)
    tm = lax.axis_index("tm")
    flag = (tm == 3).astype(jnp.int32).reshape(1)

    active = (0, 2, 3)

    def lend(t, b, j):
        return (3, b, j)

    def along_lon(steps):
        return lambda t, b, j: (t, b, (j + steps) % tiles)

    geo_own = geometry(*rest)
    geo = jnp.where(tm == 3, move(geo_own, lend, (1,)), geo_own)
    m = matrices(geo, 3 * cols)

    def neighbours(own, west_half):
        return move(own, along_lon(1), active), move(west_half, along_lon(-1), active)

    edge, inner = (0, 1, rows - 2, rows - 1), tuple(range(2, rows - 2))
    raw, _, east = split_rows(flat, edge, padded)
    far = move(east, along_lon(2), (0, 1, 2))
    own, west_half, _ = choose(flag, move(raw, lend, (1,)), raw, east, ())
    west, near = neighbours(own, west_half)
    raw_in, _, east_in = split_rows(flat, inner, padded, (own,))
    lent_in = move(raw_in, lend, (1,))
    own_in, west_half_in, east_in = choose(flag, lent_in, raw_in, east_in, (near, geo))
    far_in = move(east_in, along_lon(2), (0, 1, 2))
    west_in, near_in = neighbours(own_in, west_half_in)

    far_lent = move(far, lend, (1,))
    top, bot = lon_rows(flag, far, far_lent, near, west, own, m, ((0, 0), (2, rows - 2)), 2)
    above = move(bot, lambda t, b, j: (t, b + 1, j) if b + 1 < bands else None, active)
    below = move(top, lambda t, b, j: (t, b - 1, j) if b > 0 else None, active)
    behind, above = lax.optimization_barrier((far_in, above))
    far_lent_in = move(behind, lend, (1,))
    (mid,) = lon_rows(flag, far_in, far_lent_in, near_in, west_in, own_in, m, ((0, 2),), rows - 4, (top,))
    end = lat_rows(above, top, mid, bot, below, geo, depth)
    previous = move(end, lambda t, b, j: ({0: 1, 2: 3, 3: 2}[t], b, j), active)
    misfit = (flat.astype(jnp.float32) - previous.astype(jnp.float32)).astype(jnp.bfloat16)
    return misfit.reshape(state.shape)


def solution(mesh):
    placed = (
        P("tm", None, None, "lat", "lon"),
        P("tm", "lat"),
        P("tm", "lat", "lon", None),
        P("tm", "lat", "lon"),
        P("tm", "lat", "lon"),
        P("tm", "lat", "lon"),
        P("tm", "lat", "lon"),
        P("tm", "lat", "lon"),
    )
    return jax.shard_map(
        body,
        mesh=mesh,
        in_specs=placed,
        out_specs=P("tm", None, None, "lat", "lon"),
        check_vma=False,
    )
```

```python
import functools

import jax
import jax.numpy as jnp
from jax import lax
from jax.experimental import pallas as pl
from jax.experimental.pallas import tpu as pltpu
from jax.sharding import PartitionSpec as P

BLK = 128
AXES = ("tm", "lat", "lon")
VMEM_LIMIT = 14 * 1024 * 1024
LONG = pl.CostEstimate(flops=10**11, bytes_accessed=1000, transcendentals=0)
SHORT = pl.CostEstimate(flops=1000, bytes_accessed=1000, transcendentals=0)
VMEM = pl.BlockSpec(memory_space=pltpu.VMEM)


def params():
    return pltpu.CompilerParams(vmem_limit_bytes=VMEM_LIMIT)


def cubic(s):
    return (
        -s * (s - 1.0) * (s - 2.0) / 6.0,
        (s + 1.0) * (s - 1.0) * (s - 2.0) / 2.0,
        -(s + 1.0) * s * (s - 2.0) / 2.0,
        (s + 1.0) * s * (s - 1.0) / 6.0,
    )


def move(value, dest, windows):
    bands, tiles = lax.axis_size("lat"), lax.axis_size("lon")
    pairs = []
    for t in windows:
        for b in range(bands):
            for j in range(tiles):
                to = dest(t, b, j)
                if to is not None:
                    source = (t * bands + b) * tiles + j
                    pairs.append((source, (to[0] * bands + to[1]) * tiles + to[2]))
    return lax.ppermute(value, AXES, pairs)


def split_kernel(x_ref, *refs):
    *outs, wide_west, wide_east = refs
    depth, rows, cols = x_ref.shape
    padded = outs[0].shape[1]
    for g, buf in enumerate((wide_west, wide_east)):
        lanes = slice(g * BLK, (g + 1) * BLK)
        buf[: depth * rows] = x_ref[:, :, lanes].astype(jnp.float32).reshape(depth * rows, BLK)
        if padded > depth:
            buf[depth * rows :] = jnp.zeros(((padded - depth) * rows, BLK), jnp.float32)
        for picked, whole_ref, east_ref in zip(row_sets(rows), outs[:2], outs[2:]):
            for i, r in enumerate(picked):
                slab = buf[pl.ds(r, padded, stride=rows), :].astype(jnp.bfloat16)
                whole_ref[i, :, lanes] = slab
                if g == 1:
                    east_ref[i] = slab


def row_sets(rows):
    return (0, 1, rows - 2, rows - 1), tuple(range(2, rows - 2))


def split_rows(x, padded):
    _, rows, cols = x.shape
    edge, inner = row_sets(rows)
    shapes = [(len(picked), padded, w) for w in (cols, cols // 2) for picked in (edge, inner)]
    return pl.pallas_call(
        split_kernel,
        out_shape=[jax.ShapeDtypeStruct(shape, x.dtype) for shape in shapes],
        in_specs=[VMEM],
        out_specs=[VMEM] * 4,
        scratch_shapes=[pltpu.VMEM((padded * rows, BLK), jnp.float32)] * 2,
        compiler_params=params(),
        cost_estimate=SHORT,
        name="split_rows",
    )(x)


def choose_kernel(lent_flag, lent_ref, own_ref, own_east_ref, *refs):
    whole_ref, west_ref, east_ref = refs[-3:]
    half = west_ref.shape[2]
    east_ref[...] = own_east_ref[...]
    for flag, ref in enumerate((own_ref, lent_ref)):

        @pl.when(lent_flag[0] == flag)
        def _():
            whole_ref[...] = ref[...]
            west_ref[...] = ref[:, :, :half]


def choose(flag, lent, own, own_east, after):
    count, depth, cols = own.shape
    half = jax.ShapeDtypeStruct(own_east.shape, own.dtype)

    def block(width, index):
        return pl.BlockSpec((1, depth, width), index)

    def each(i, flag_ref):
        return (i, 0, 0)

    return pl.pallas_call(
        choose_kernel,
        grid_spec=pltpu.PrefetchScalarGridSpec(
            num_scalar_prefetch=1,
            grid=(count,),
            in_specs=[
                block(cols, lambda i, flag_ref: (i * flag_ref[0], 0, 0)),
                block(cols, lambda i, flag_ref: (i * (1 - flag_ref[0]), 0, 0)),
                block(cols // 2, each),
            ]
            + [pl.BlockSpec(memory_space=pl.ANY)] * len(after),
            out_specs=[block(cols, each), block(cols // 2, each), block(cols // 2, each)],
        ),
        out_shape=(jax.ShapeDtypeStruct(own.shape, own.dtype), half, half),
        compiler_params=params(),
        cost_estimate=SHORT,
        name="choose",
    )(flag, lent, own, own_east, *after)


def token_kernel(*refs):
    refs[-1][...] = jnp.zeros_like(refs[-1])


def token(*after):
    return pl.pallas_call(
        token_kernel,
        out_shape=jax.ShapeDtypeStruct((8, BLK), jnp.float32),
        in_specs=[pl.BlockSpec(memory_space=pl.ANY)] * len(after),
        out_specs=VMEM,
        compiler_params=params(),
        cost_estimate=LONG,
        name="token",
    )(*after)


def matrix_kernel(geo_ref, m_ref):
    r = pl.program_id(0)
    _, span, cols = m_ref.shape
    first = geo_ref[0, pl.ds(r, 1), :].astype(jnp.int32)
    weights = [w.astype(jnp.bfloat16).astype(jnp.float32) for w in cubic(geo_ref[1, pl.ds(r, 1), :])]
    step = BLK // 2
    for s in range(0, span, step):
        gap = lax.broadcasted_iota(jnp.int32, (step, cols), 0) - (first - s)
        value = jnp.where(gap == 0, weights[0], 0.0)
        for node in range(1, 4):
            value = jnp.where(gap == node, weights[node], value)
        m_ref[0, s : s + step, :] = value.astype(jnp.bfloat16)


def matrices(geo, span):
    _, rows, cols = geo.shape
    return pl.pallas_call(
        matrix_kernel,
        grid=(rows,),
        out_shape=jax.ShapeDtypeStruct((rows, span, cols), jnp.bfloat16),
        in_specs=[pl.BlockSpec(geo.shape, lambda r: (0, 0, 0))],
        out_specs=pl.BlockSpec((1, span, cols), lambda r: (r, 0, 0)),
        compiler_params=params(),
        cost_estimate=SHORT,
        name="matrices",
    )(geo)


def row_product(far, near, west, own, m):
    outer = jnp.concatenate([far, near], axis=1)
    k = outer.shape[1]
    f32 = jnp.float32
    total = jnp.dot(outer, m[:k], preferred_element_type=f32)
    total += jnp.dot(west, m[k : 2 * k], preferred_element_type=f32)
    total += jnp.dot(own, m[2 * k :], preferred_element_type=f32)
    return total.astype(jnp.bfloat16)


def lon_kernel(lent_flag, *refs, per_step):
    ins, outs = refs[: 6 * per_step], refs[len(refs) - per_step :]
    lent = lent_flag[0] == 1
    for k in range(per_step):
        far, far_lent, near, west, own, m = ins[6 * k : 6 * k + 6]
        second_west = jnp.where(lent, far_lent[0], far[0])
        outs[k][0] = row_product(second_west, near[0], west[0], own[0], m[0])


def lon_rows(flag, far, far_lent, near, west, own, m, firsts, count, after=()):
    _, depth, cols = own.shape
    arrays = (far, far_lent, near, west, own)

    def at(array, first):
        return pl.BlockSpec((1,) + array.shape[1:], lambda i, first=first: (i + first, 0, 0))

    specs = []
    for slab, row in firsts:
        specs += [at(array, slab) for array in arrays] + [at(m, row)]
    return pl.pallas_call(
        functools.partial(lon_kernel, per_step=len(firsts)),
        grid=(count,),
        out_shape=[jax.ShapeDtypeStruct((count, depth, cols), jnp.bfloat16) for _ in firsts],
        in_specs=[pl.BlockSpec(memory_space=pltpu.SMEM)] + specs + [pl.BlockSpec(memory_space=pl.ANY)] * len(after),
        out_specs=[pl.BlockSpec((1, depth, cols), lambda i: (i, 0, 0)) for _ in firsts],
        compiler_params=params(),
        cost_estimate=SHORT,
        name="lon_rows",
    )(flag, *((*arrays, m) * len(firsts)), *after)


def lat_kernel(above, top, mid, bot, below, geo_ref, out_ref, *wide):
    depth, rows, cols = out_ref.shape
    chunk = 48
    shift, weights = geo_ref[2].astype(jnp.int32), cubic(geo_ref[3])
    coefficients = []
    for distance in range(-2, 3):
        total = jnp.zeros_like(weights[0])
        for node in range(4):
            total += jnp.where(shift + node - 1 == distance, weights[node], 0.0)
        coefficients.append(total)
    padded = [(ref, i) for ref in (above, top, mid, bot, below) for i in range(ref.shape[0])]
    for low in range(0, depth, chunk):
        size = min(chunk, depth - low)
        for r in range(rows):
            total = None
            for k in range(5):
                ref, i = padded[r + k]
                term = coefficients[k][r : r + 1] * ref[i, low : low + size, :].astype(jnp.float32)
                total = term if total is None else total + term
            for g, buf in enumerate(wide):
                buf[pl.ds(low * rows + r, size, stride=rows), :] = total[:, g * BLK : (g + 1) * BLK]
        for g, buf in enumerate(wide):
            block = buf[low * rows : (low + size) * rows, :].astype(jnp.bfloat16)
            out_ref[low : low + size, :, g * BLK : (g + 1) * BLK] = block.reshape(size, rows, BLK)


def lat_rows(above, top, mid, bot, below, geo, depth):
    cols = mid.shape[2]
    rows = geo.shape[1]
    return pl.pallas_call(
        lat_kernel,
        out_shape=jax.ShapeDtypeStruct((depth, rows, cols), jnp.bfloat16),
        in_specs=[VMEM] * 6,
        out_specs=VMEM,
        scratch_shapes=[pltpu.VMEM((depth * rows, BLK), jnp.float32)] * (cols // BLK),
        compiler_params=params(),
        cost_estimate=SHORT,
        name="lat_rows",
    )(above, top, mid, bot, below, geo)


def geometry(band_counts, dep_blocks, lon_entry, lon_offset, lon_frac, lat_offset, lat_frac):
    blocks, kmax = dep_blocks.shape[2:]
    cycle = blocks * lax.axis_size("lon")
    count, entry = band_counts[0, 0], lon_entry[0]
    slot = entry % count
    place = (dep_blocks[0] - lax.axis_index("lon") * blocks + blocks + blocks // 2) % cycle
    place = jnp.where(place == 0, 0, jnp.where(place == 3 * blocks - 1, 1, place + 1))
    place = jnp.repeat(place, BLK, axis=1)
    chosen = place[:, :, 0]
    for k in range(1, kmax):
        chosen = jnp.where(slot == k, place[:, :, k], chosen)
    first = chosen * BLK + lon_offset[0] - 1
    return jnp.stack(
        [first.astype(jnp.float32), lon_frac[0], lat_offset[0].astype(jnp.float32), lat_frac[0]]
    )


def body(state, *rest):
    fields_n, levels, rows, cols = state.shape[1:]
    depth = fields_n * levels
    padded = -(-depth // 8) * 8
    _, bands, tiles = (lax.axis_size(a) for a in AXES)
    flat = state.reshape(depth, rows, cols)
    tm = lax.axis_index("tm")
    flag = (tm == 3).astype(jnp.int32).reshape(1)

    active = (0, 2, 3)

    def lend(t, b, j):
        return (3, b, j)

    def along_lon(steps):
        return lambda t, b, j: (t, b, (j + steps) % tiles)

    geo_own = geometry(*rest)
    geo = jnp.where(tm == 3, move(geo_own, lend, (1,)), geo_own)
    m = matrices(geo, 3 * cols)

    def neighbours(own, west_half):
        return move(own, along_lon(1), active), move(west_half, along_lon(-1), active)

    raw, raw_in, east, east_in = split_rows(flat, padded)
    far = move(east, along_lon(2), (0, 1, 2))
    own, west_half, _ = choose(flag, move(raw, lend, (1,)), raw, east, ())
    west, near = neighbours(own, west_half)
    lent_in = move(raw_in, lend, (1,))
    own_in, west_half_in, east_in = choose(flag, lent_in, raw_in, east_in, (near, geo))
    far_in = move(east_in, along_lon(2), (0, 1, 2))
    west_in, near_in = neighbours(own_in, west_half_in)

    far_lent = move(far, lend, (1,))
    top, bot = lon_rows(flag, far, far_lent, near, west, own, m, ((0, 0), (2, rows - 2)), 2)
    above = move(bot, lambda t, b, j: (t, b + 1, j) if b + 1 < bands else None, active)
    below = move(top, lambda t, b, j: (t, b - 1, j) if b > 0 else None, active)
    behind, top = lax.optimization_barrier((far_in, top))
    far_lent_in = move(behind, lend, (1,))
    (mid,) = lon_rows(flag, far_in, far_lent_in, near_in, west_in, own_in, m, ((0, 2),), rows - 4, (top,))
    end = lat_rows(above, top, mid, bot, below, geo, depth)
    previous = move(end, lambda t, b, j: ({0: 1, 2: 3, 3: 2}[t], b, j), active)
    misfit = (flat.astype(jnp.float32) - previous.astype(jnp.float32)).astype(jnp.bfloat16)
    return misfit.reshape(state.shape)


def solution(mesh):
    placed = (
        P("tm", None, None, "lat", "lon"),
        P("tm", "lat"),
        P("tm", "lat", "lon", None),
        P("tm", "lat", "lon"),
        P("tm", "lat", "lon"),
        P("tm", "lat", "lon"),
        P("tm", "lat", "lon"),
        P("tm", "lat", "lon"),
    )
    return jax.shard_map(
        body,
        mesh=mesh,
        in_specs=placed,
        out_specs=P("tm", None, None, "lat", "lon"),
        check_vma=False,
    )
```

```python
import functools

import jax
import jax.numpy as jnp
from jax import lax
from jax.experimental import pallas as pl
from jax.experimental.pallas import tpu as pltpu
from jax.sharding import PartitionSpec as P

BLK = 128
AXES = ("tm", "lat", "lon")
VMEM_LIMIT = 14 * 1024 * 1024
LONG = pl.CostEstimate(flops=10**11, bytes_accessed=1000, transcendentals=0)
SHORT = pl.CostEstimate(flops=1000, bytes_accessed=1000, transcendentals=0)
VMEM = pl.BlockSpec(memory_space=pltpu.VMEM)


def params():
    return pltpu.CompilerParams(vmem_limit_bytes=VMEM_LIMIT)


def cubic(s):
    return (
        -s * (s - 1.0) * (s - 2.0) / 6.0,
        (s + 1.0) * (s - 1.0) * (s - 2.0) / 2.0,
        -(s + 1.0) * s * (s - 2.0) / 2.0,
        (s + 1.0) * s * (s - 1.0) / 6.0,
    )


def move(value, dest, windows):
    bands, tiles = lax.axis_size("lat"), lax.axis_size("lon")
    pairs = []
    for t in windows:
        for b in range(bands):
            for j in range(tiles):
                to = dest(t, b, j)
                if to is not None:
                    source = (t * bands + b) * tiles + j
                    pairs.append((source, (to[0] * bands + to[1]) * tiles + to[2]))
    return lax.ppermute(value, AXES, pairs)


def split_kernel(x_ref, *refs):
    *outs, wide_west, wide_east = refs
    depth, rows, cols = x_ref.shape
    padded = outs[0].shape[1]
    for g, buf in enumerate((wide_west, wide_east)):
        lanes = slice(g * BLK, (g + 1) * BLK)
        buf[: depth * rows] = x_ref[:, :, lanes].astype(jnp.float32).reshape(depth * rows, BLK)
        if padded > depth:
            buf[depth * rows :] = jnp.zeros(((padded - depth) * rows, BLK), jnp.float32)
        for picked, whole_ref, east_ref in zip(row_sets(rows), outs[:2], outs[2:]):
            for i, r in enumerate(picked):
                slab = buf[pl.ds(r, padded, stride=rows), :].astype(jnp.bfloat16)
                whole_ref[i, :, lanes] = slab
                if g == 1:
                    east_ref[i] = slab


def row_sets(rows):
    return (0, 1, rows - 2, rows - 1), tuple(range(2, rows - 2))


def split_rows(x, padded):
    _, rows, cols = x.shape
    edge, inner = row_sets(rows)
    shapes = [(len(picked), padded, w) for w in (cols, cols // 2) for picked in (edge, inner)]
    return pl.pallas_call(
        split_kernel,
        out_shape=[jax.ShapeDtypeStruct(shape, x.dtype) for shape in shapes],
        in_specs=[VMEM],
        out_specs=[VMEM] * 4,
        scratch_shapes=[pltpu.VMEM((padded * rows, BLK), jnp.float32)] * 2,
        compiler_params=params(),
        cost_estimate=SHORT,
        name="split_rows",
    )(x)


def choose_kernel(lent_flag, lent_ref, own_ref, own_east_ref, *refs):
    whole_ref, west_ref, east_ref = refs[-3:]
    half = west_ref.shape[2]
    east_ref[...] = own_east_ref[...]
    for flag, ref in enumerate((own_ref, lent_ref)):

        @pl.when(lent_flag[0] == flag)
        def _():
            whole_ref[...] = ref[...]
            west_ref[...] = ref[:, :, :half]


def choose(flag, lent, own, own_east, after):
    count, depth, cols = own.shape
    half = jax.ShapeDtypeStruct(own_east.shape, own.dtype)

    def block(width, index):
        return pl.BlockSpec((1, depth, width), index)

    def each(i, flag_ref):
        return (i, 0, 0)

    return pl.pallas_call(
        choose_kernel,
        grid_spec=pltpu.PrefetchScalarGridSpec(
            num_scalar_prefetch=1,
            grid=(count,),
            in_specs=[
                block(cols, lambda i, flag_ref: (i * flag_ref[0], 0, 0)),
                block(cols, lambda i, flag_ref: (i * (1 - flag_ref[0]), 0, 0)),
                block(cols // 2, each),
            ]
            + [pl.BlockSpec(memory_space=pl.ANY)] * len(after),
            out_specs=[block(cols, each), block(cols // 2, each), block(cols // 2, each)],
        ),
        out_shape=(jax.ShapeDtypeStruct(own.shape, own.dtype), half, half),
        compiler_params=params(),
        cost_estimate=SHORT,
        name="choose",
    )(flag, lent, own, own_east, *after)


def token_kernel(*refs):
    refs[-1][...] = jnp.zeros_like(refs[-1])


def token(*after):
    return pl.pallas_call(
        token_kernel,
        out_shape=jax.ShapeDtypeStruct((8, BLK), jnp.float32),
        in_specs=[pl.BlockSpec(memory_space=pl.ANY)] * len(after),
        out_specs=VMEM,
        compiler_params=params(),
        cost_estimate=LONG,
        name="token",
    )(*after)


def matrix_kernel(geo_ref, m_ref):
    r = pl.program_id(0)
    _, span, cols = m_ref.shape
    first = geo_ref[0, pl.ds(r, 1), :].astype(jnp.int32)
    weights = [w.astype(jnp.bfloat16).astype(jnp.float32) for w in cubic(geo_ref[1, pl.ds(r, 1), :])]
    step = BLK // 2
    for s in range(0, span, step):
        gap = lax.broadcasted_iota(jnp.int32, (step, cols), 0) - (first - s)
        value = jnp.where(gap == 0, weights[0], 0.0)
        for node in range(1, 4):
            value = jnp.where(gap == node, weights[node], value)
        m_ref[0, s : s + step, :] = value.astype(jnp.bfloat16)


def matrices(geo, span):
    _, rows, cols = geo.shape
    return pl.pallas_call(
        matrix_kernel,
        grid=(rows,),
        out_shape=jax.ShapeDtypeStruct((rows, span, cols), jnp.bfloat16),
        in_specs=[pl.BlockSpec(geo.shape, lambda r: (0, 0, 0))],
        out_specs=pl.BlockSpec((1, span, cols), lambda r: (r, 0, 0)),
        compiler_params=params(),
        cost_estimate=SHORT,
        name="matrices",
    )(geo)


def row_product(far, near, west, own, m):
    outer = jnp.concatenate([far, near], axis=1)
    k = outer.shape[1]
    f32 = jnp.float32
    total = jnp.dot(outer, m[:k], preferred_element_type=f32)
    total += jnp.dot(west, m[k : 2 * k], preferred_element_type=f32)
    total += jnp.dot(own, m[2 * k :], preferred_element_type=f32)
    return total.astype(jnp.bfloat16)


def lon_kernel(lent_flag, *refs, per_step):
    ins, outs = refs[: 6 * per_step], refs[len(refs) - per_step :]
    lent = lent_flag[0] == 1
    for k in range(per_step):
        far, far_lent, near, west, own, m = ins[6 * k : 6 * k + 6]
        second_west = jnp.where(lent, far_lent[0], far[0])
        outs[k][0] = row_product(second_west, near[0], west[0], own[0], m[0])


def lon_rows(flag, far, far_lent, near, west, own, m, firsts, count, after=()):
    _, depth, cols = own.shape
    arrays = (far, far_lent, near, west, own)

    def at(array, first):
        return pl.BlockSpec((1,) + array.shape[1:], lambda i, first=first: (i + first, 0, 0))

    specs = []
    for slab, row in firsts:
        specs += [at(array, slab) for array in arrays] + [at(m, row)]
    return pl.pallas_call(
        functools.partial(lon_kernel, per_step=len(firsts)),
        grid=(count,),
        out_shape=[jax.ShapeDtypeStruct((count, depth, cols), jnp.bfloat16) for _ in firsts],
        in_specs=[pl.BlockSpec(memory_space=pltpu.SMEM)] + specs + [pl.BlockSpec(memory_space=pl.ANY)] * len(after),
        out_specs=[pl.BlockSpec((1, depth, cols), lambda i: (i, 0, 0)) for _ in firsts],
        compiler_params=params(),
        cost_estimate=SHORT,
        name="lon_rows",
    )(flag, *((*arrays, m) * len(firsts)), *after)


def lat_kernel(above, top, mid, bot, below, geo_ref, out_ref, *wide):
    depth, rows, cols = out_ref.shape
    chunk = 48
    shift, weights = geo_ref[2].astype(jnp.int32), cubic(geo_ref[3])
    coefficients = []
    for distance in range(-2, 3):
        total = jnp.zeros_like(weights[0])
        for node in range(4):
            total += jnp.where(shift + node - 1 == distance, weights[node], 0.0)
        coefficients.append(total)
    padded = [(ref, i) for ref in (above, top, mid, bot, below) for i in range(ref.shape[0])]
    for low in range(0, depth, chunk):
        size = min(chunk, depth - low)
        for r in range(rows):
            total = None
            for k in range(5):
                ref, i = padded[r + k]
                term = coefficients[k][r : r + 1] * ref[i, low : low + size, :].astype(jnp.float32)
                total = term if total is None else total + term
            for g, buf in enumerate(wide):
                buf[pl.ds(low * rows + r, size, stride=rows), :] = total[:, g * BLK : (g + 1) * BLK]
        for g, buf in enumerate(wide):
            block = buf[low * rows : (low + size) * rows, :].astype(jnp.bfloat16)
            out_ref[low : low + size, :, g * BLK : (g + 1) * BLK] = block.reshape(size, rows, BLK)


def lat_rows(above, top, mid, bot, below, geo, depth):
    cols = mid.shape[2]
    rows = geo.shape[1]
    return pl.pallas_call(
        lat_kernel,
        out_shape=jax.ShapeDtypeStruct((depth, rows, cols), jnp.bfloat16),
        in_specs=[VMEM] * 6,
        out_specs=VMEM,
        scratch_shapes=[pltpu.VMEM((depth * rows, BLK), jnp.float32)] * (cols // BLK),
        compiler_params=params(),
        cost_estimate=SHORT,
        name="lat_rows",
    )(above, top, mid, bot, below, geo)


def geometry(band_counts, dep_blocks, lon_entry, lon_offset, lon_frac, lat_offset, lat_frac):
    blocks, kmax = dep_blocks.shape[2:]
    cycle = blocks * lax.axis_size("lon")
    count, entry = band_counts[0, 0], lon_entry[0]
    slot = entry % count
    place = (dep_blocks[0] - lax.axis_index("lon") * blocks + blocks + blocks // 2) % cycle
    place = jnp.where(place == 0, 0, jnp.where(place == 3 * blocks - 1, 1, place + 1))
    place = jnp.repeat(place, BLK, axis=1)
    chosen = place[:, :, 0]
    for k in range(1, kmax):
        chosen = jnp.where(slot == k, place[:, :, k], chosen)
    first = chosen * BLK + lon_offset[0] - 1
    return jnp.stack(
        [first.astype(jnp.float32), lon_frac[0], lat_offset[0].astype(jnp.float32), lat_frac[0]]
    )


def body(state, *rest):
    fields_n, levels, rows, cols = state.shape[1:]
    depth = fields_n * levels
    padded = -(-depth // 8) * 8
    _, bands, tiles = (lax.axis_size(a) for a in AXES)
    flat = state.reshape(depth, rows, cols)
    tm = lax.axis_index("tm")
    flag = (tm == 3).astype(jnp.int32).reshape(1)

    active = (0, 2, 3)

    def lend(t, b, j):
        return (3, b, j)

    def along_lon(steps):
        return lambda t, b, j: (t, b, (j + steps) % tiles)

    geo_own = geometry(*rest)
    geo = jnp.where(tm == 3, move(geo_own, lend, (1,)), geo_own)
    m = matrices(geo, 3 * cols)

    def neighbours(own, west_half):
        return move(own, along_lon(1), active), move(west_half, along_lon(-1), active)

    raw, raw_in, east, east_in = split_rows(flat, padded)
    far = move(east, along_lon(2), (0, 1, 2))
    own, west_half, _ = choose(flag, move(raw, lend, (1,)), raw, east, ())
    west, near = neighbours(own, west_half)
    lent_in = move(raw_in, lend, (1,))
    own_in, west_half_in, east_in = choose(flag, lent_in, raw_in, east_in, (near, geo))
    far_in = move(east_in, along_lon(2), (0, 1, 2))
    west_in, near_in = neighbours(own_in, west_half_in)

    far_lent = move(far, lend, (1,))
    top, bot = lon_rows(flag, far, far_lent, near, west, own, m, ((0, 0), (2, rows - 2)), 2)
    above = move(bot, lambda t, b, j: (t, b + 1, j) if b + 1 < bands else None, active)
    below = move(top, lambda t, b, j: (t, b - 1, j) if b > 0 else None, active)
    behind = far_in
    far_lent_in = move(behind, lend, (1,))
    (mid,) = lon_rows(flag, far_in, far_lent_in, near_in, west_in, own_in, m, ((0, 2),), rows - 4, (top,))
    end = lat_rows(above, top, mid, bot, below, geo, depth)
    previous = move(end, lambda t, b, j: ({0: 1, 2: 3, 3: 2}[t], b, j), active)
    misfit = (flat.astype(jnp.float32) - previous.astype(jnp.float32)).astype(jnp.bfloat16)
    return misfit.reshape(state.shape)


def solution(mesh):
    placed = (
        P("tm", None, None, "lat", "lon"),
        P("tm", "lat"),
        P("tm", "lat", "lon", None),
        P("tm", "lat", "lon"),
        P("tm", "lat", "lon"),
        P("tm", "lat", "lon"),
        P("tm", "lat", "lon"),
        P("tm", "lat", "lon"),
    )
    return jax.shard_map(
        body,
        mesh=mesh,
        in_specs=placed,
        out_specs=P("tm", None, None, "lat", "lon"),
        check_vma=False,
    )
```
